32 devices in a mesh: group: 2 (over y), depth: 8 (over z, x), tile: 2 (over core).
Axes of the slice: x: 2, y: 2, z: 4, core: 2. Of those that a mesh axis runs over, the one named last changes fastest.
Arguments:
- volume: bfloat16 [8, 6, 64, 8, 256], P('depth', None, 'group', None, 'tile'), parts along dimension 2, may hold values from -6 to 6
- dw_weight: bfloat16 [32, 7, 7, 7], replicated, may hold values from -0.3125 to 0.3125
- up_weight: bfloat16 [128, 32], replicated, may hold values from -1 to 1
- down_weight: bfloat16 [32, 128], replicated, may hold values from -0.5 to 0.5
- tap_weight: bfloat16 [3, 32, 32], replicated, may hold values from -0.625 to 0.625
- opacity_weight: float32 [32], replicated, may hold values from -1 to 1
- decode_weight: bfloat16 [32, 32, 3, 3], replicated, may hold values from -0.375 to 0.375
- out_weight: bfloat16 [3, 32], replicated, may hold values from -1 to 1
Outputs:
- rgb: float32 [6, 16, 256], P('group', 'depth', 'tile'), parts along dimension 0
The draws below stay inside these ranges and needn't reach their ends.
There are 2 independent parts, one for each index of `group`. The reference program is written for one: setup_inputs(seed, part) draws one part's arguments, and reference() takes and returns one part's arrays. A program takes and returns all parts, laid end to end along the dimension named above; an argument that names none is the same for every part. Nothing has to cross between parts.
All inputs are finite; a program needn't handle non-finite values.
Results may differ from the reference program's by a relative error of at most 0.012.
Values may be sent and summed in bfloat16 or wider, within the bound.
A program may use at most 64 MiB of HBM per device.

```python
import jax
import jax.numpy as jnp
from jax import lax

C = 32
HID = 128
CZ = 6
ROW_BAND = 8
BANDS = 2
SLABS = 4
NZ = 24
H = 16
W = 256
N_DEPTH = 8


def levels(stream_key, dims, cuts, low, top_value):
    factor_of, own = 1.0, jax.random.fold_in(stream_key, 6)
    for dim, shards_of in cuts:
        draws = jnp.exp(jax.random.uniform(jax.random.fold_in(own, dim), (shards_of,), jnp.float32, low / len(cuts), top_value / len(cuts)))
        factor_of = factor_of * jnp.repeat(draws, dims[dim] // shards_of).reshape([-1 if axis == dim else 1 for axis in range(len(dims))])
    return factor_of


def noise(own_key, dims, scale, bound, split=(), dtype=jnp.bfloat16):
    gain = levels(own_key, dims, split, -0.22, 0.18) if split else 1.0
    drawn = jax.random.normal(own_key, dims, jnp.float32) * scale * gain
    return jnp.minimum(jnp.maximum(drawn, -bound), bound).astype(dtype)


def setup_inputs(seed: int = 0, part: int = 0) -> dict:
    key_of = jax.random.split(jax.random.key(seed), 9)
    part_splits = jax.random.split(jax.random.fold_in(key_of[8], part), 9)
    volume = noise(part_splits[0], (N_DEPTH, CZ, C, ROW_BAND, W), 1.0, 6.0, ((0, 8), (4, 2)))
    dw_weight = noise(key_of[1], (C, 7, 7, 7), 343 ** -0.5, 0.3125)
    up_weight = noise(key_of[2], (HID, C), C ** -0.5, 1.0)
    down_weight = noise(key_of[3], (C, HID), HID ** -0.5, 0.5)
    tap_weight = noise(key_of[4], (3, C, C), (3 * C) ** -0.5, 0.625)
    opacity_weight = noise(key_of[5], (C,), C ** -0.5, 1.0, (), jnp.float32)
    decode_weight = noise(key_of[6], (C, C, 3, 3), (9 * C) ** -0.5, 0.375)
    out_weight = noise(key_of[7], (3, C), C ** -0.5, 1.0)
    return {"volume": volume, "dw_weight": dw_weight, "up_weight": up_weight, "down_weight": down_weight, "tap_weight": tap_weight, "opacity_weight": opacity_weight, "decode_weight": decode_weight, "out_weight": out_weight}


def reference(volume, dw_weight, up_weight, down_weight, tap_weight, opacity_weight, decode_weight, out_weight):
    channels = volume.shape[2]
    blocks = volume.reshape((SLABS, BANDS) + volume.shape[1:])
    grid = jnp.transpose(blocks, (0, 2, 3, 1, 4, 5)).reshape(NZ, channels, H, volume.shape[4])
    spread = lax.conv_general_dilated(grid[None], dw_weight[:, None], (1, 1, 1), ((3, 3), (3, 3), (3, 3)), dimension_numbers=('NDCHW', 'OIDHW', 'NDCHW'), feature_group_count=channels, preferred_element_type=jnp.float32)[0]

    def mix_plane(item):
        spread_plane, plane = item
        square = lax.optimization_barrier(jnp.mean(spread_plane * spread_plane, axis=0))
        normed = (spread_plane * lax.rsqrt(square + 1e-05)).astype(jnp.bfloat16)
        flat = normed.reshape(channels, -1)
        hidden = jax.nn.gelu(jnp.dot(up_weight, flat, preferred_element_type=jnp.float32)).astype(jnp.bfloat16)
        delta = jnp.dot(down_weight, hidden, preferred_element_type=jnp.float32).reshape(plane.shape)
        return (plane.astype(jnp.float32) + delta).astype(jnp.bfloat16)
    mixed = lax.map(mix_plane, (spread, grid))
    framed = jnp.pad(mixed, ((1, 1), (0, 0), (0, 0), (0, 0)))
    scale = 4.0 / NZ

    def march(carry, plane_index):
        light, color = carry
        window = lax.dynamic_slice_in_dim(framed, plane_index, 3, 0)
        glow = jnp.einsum('koc,kchw->ohw', tap_weight.astype(jnp.float32), window.astype(jnp.float32))
        logit = lax.optimization_barrier(jnp.sum(opacity_weight[:, None, None] * glow, axis=0))
        alpha = scale * jax.nn.sigmoid(logit)
        color = color + (light * alpha)[None] * glow
        light = light * (1.0 - alpha)
        return ((light, color), None)
    start = (jnp.ones(grid.shape[2:], jnp.float32), jnp.zeros(grid.shape[1:], jnp.float32))
    (light, image), unused = lax.scan(march, start, jnp.arange(grid.shape[0]).astype(jnp.int32))
    square = lax.optimization_barrier(jnp.mean(image * image, axis=0))
    flat_image = (image * lax.rsqrt(square + 1e-05)).astype(jnp.bfloat16)
    decoded = lax.conv_general_dilated(flat_image[None], decode_weight, (1, 1), ((1, 1), (1, 1)), dimension_numbers=('NCHW', 'OIHW', 'NCHW'), preferred_element_type=jnp.float32)[0]
    decoded = jax.nn.gelu(decoded).astype(jnp.bfloat16)
    rgb = jnp.dot(out_weight, decoded.reshape(channels, -1), preferred_element_type=jnp.float32)
    return rgb.reshape((3,) + image.shape[1:])
```

```python
import functools

import jax
import jax.numpy as jnp
from jax import lax
from jax.experimental import pallas as pl
from jax.experimental.pallas import tpu as pltpu
from jax.sharding import PartitionSpec as P

BF = jnp.bfloat16
F32 = jnp.float32
GROUPS = 4


def iota(shape, dim):
    return lax.broadcasted_iota(jnp.int32, shape, dim)


def dot(a, b):
    return jnp.dot(a, b, preferred_element_type=F32)


def gelu(x):
    return 0.5 * x * (1.0 + jnp.tanh(0.7978845608028654 * (x + 0.044715 * (x * x * x))))


def spread_rows(weight):
    m, n = weight.shape
    left = ((iota((8 * m, m), 0) >> 3) == iota((8 * m, m), 1)).astype(F32).astype(BF)
    right = (iota((n, 8 * n), 0) == (iota((n, 8 * n), 1) >> 3)).astype(F32).astype(BF)
    full = dot(dot(left, weight).astype(BF), right)
    same = (iota(full.shape, 0) & 7) == (iota(full.shape, 1) & 7)
    return jnp.where(same, full, 0.0).astype(BF)


def shift_sum(main, halo, taps, rows):
    lane = iota((rows, 128), 1)
    total = None
    for k in range(taps):
        s = k - taps // 2
        m = main[k * rows : (k + 1) * rows]
        if s:
            h = halo[k * rows : (k + 1) * rows]
            pick = lane < s if s > 0 else lane >= 128 + s
            m = pltpu.roll(jnp.where(pick, h, m), (128 - s) % 128, 1)
        total = m if total is None else total + m
    return total


def kernel(
    bands, slabs,
    vol, taps, up, down, tap, opacity, dec, outw,
    rgb,
    front, back, upo, dno, belo, abov, base, toep, xs, xh, spread, ku, kd, kt,
    mixed, color, pieces, gathered, flat, near,
    plane_s, plane_r, row_s, row_r, col_s, col_r, mix_s, mix_r, comp_s, comp_r, img_s, img_r,
):
    planes = vol.shape[0]
    g = lax.axis_index("group")
    me = lax.axis_index("depth")
    t = lax.axis_index("tile")
    slab, band = me // bands, me % bands
    count = bands * slabs
    r = 8 // slabs
    other = 1 - t

    def at(position, tile):
        return (g, position, tile)

    has = {
        "next": slab < slabs - 1, "prev": slab > 0,
        "below": band < bands - 1, "above": band > 0,
        "after": me < count - 1, "before": me > 0,
    }
    bar = pltpu.get_barrier_semaphore()

    def greet(position, tile):
        pl.semaphore_signal(
            bar, inc=1, device_id=at(position, tile), device_id_type=pl.DeviceIdType.MESH
        )

    def both(cond, fn):
        pl.when(cond)(fn)

    greet(me, other)
    both(has["next"], lambda: greet(me + bands, t))
    both(has["prev"], lambda: greet(me - bands, t))
    both(has["below"], lambda: greet(me + 1, t))
    both(has["above"], lambda: greet(me - 1, t))
    for q in range(2):
        tile = t if q == 0 else other
        both(has["after"], lambda tile=tile: greet(me + 1, tile))
        both(has["before"], lambda tile=tile: greet(me - 1, tile))
    my_band, my_piece = me // slabs, me % slabs
    for s in range(slabs):
        src = s * bands + my_band
        both(src != me, lambda src=src: greet(src, t))
    one, two = jnp.int32(1), jnp.int32(2)
    total = one
    for name, amount in (("next", one), ("prev", one), ("below", one), ("above", one),
                         ("after", two), ("before", two)):
        total = total + jnp.where(has[name], amount, 0)
    for j in range(slabs):
        total = total + jnp.where(band * slabs + j != me, one, 0)
    pl.semaphore_wait(bar, total)

    def copy(src, dst, ss, rs, position, tile):
        return pltpu.make_async_remote_copy(
            src_ref=src, dst_ref=dst, send_sem=ss, recv_sem=rs,
            device_id=at(position, tile), device_id_type=pl.DeviceIdType.MESH,
        )

    def zero(ref):
        ref[...] = jnp.zeros(ref.shape, ref.dtype)

    to_next = copy(vol.at[planes - 3 : planes], front, plane_s.at[0], plane_r.at[0], me + bands, t)
    to_prev = copy(vol.at[0:3], back, plane_s.at[1], plane_r.at[1], me - bands, t)
    both(has["next"], to_next.start)
    both(has["prev"], to_prev.start)

    sub = iota((16, 8, 128), 1)

    def pack_rows(ref, start, n):
        def one(i, carry):
            x = ref[i].astype(F32).reshape(16, 2, 8, 128)
            a, b = x[:, 0], x[:, 1]
            low = jnp.where(sub < 4, a, pltpu.roll(b, 4, 1))
            high = jnp.where(sub < 4, pltpu.roll(a, 4, 1), b)
            upo[start + i] = low.reshape(128, 128).astype(BF)
            dno[start + i] = high.reshape(128, 128).astype(BF)
            return carry

        lax.fori_loop(0, n, one, 0)

    def row_copies(k, start, n):
        return (
            copy(upo.at[start : start + n], belo.at[start : start + n],
                 row_s.at[0, k], row_r.at[0, k], me - 1, t),
            copy(dno.at[start : start + n], abov.at[start : start + n],
                 row_s.at[1, k], row_r.at[1, k], me + 1, t),
        )

    rows = [row_copies(0, 3, planes), row_copies(1, 0, 3), row_copies(2, 3 + planes, 3)]

    def send_rows(k):
        both(has["above"], rows[k][0].start)
        both(has["below"], rows[k][1].start)

    pack_rows(vol, 3, planes)
    send_rows(0)
    both(jnp.logical_not(has["prev"]), lambda: zero(front))
    both(jnp.logical_not(has["next"]), lambda: zero(back))
    both(jnp.logical_not(has["below"]), lambda: zero(belo))
    both(jnp.logical_not(has["above"]), lambda: zero(abov))

    def build_base():
        for h in range(8):
            row, lane = iota((64, 128), 0), iota((64, 128), 1)
            dh = ((lane & 15) - h + 3) & 15
            hit = (row == (lane >> 4) * 7 + dh) & (dh < 7) & (lane < 112)
            base[h * 224 : (h + 1) * 224] = dot(taps[...], hit.astype(F32).astype(BF))

    def build_toeplitz():
        lane = iota((8, 128), 1)

        def one(c, carry):
            for k in range(7):
                b = base[pl.ds(k * 32 + c, 8, stride=224), :]
                low, high = [], []
                for p in range(planes):
                    moved = pltpu.roll(b, 16 * p, 1) if p else b
                    low.append(jnp.where(lane >= 16 * p, moved, 0.0))
                    high.append(jnp.where(lane < 16 * p, moved, 0.0))
                toep[c, k * 48 : (k + 1) * 48, 0:128] = jnp.concatenate(low, 0).astype(BF)
                toep[c, k * 48 : (k + 1) * 48, 128:256] = jnp.concatenate(high, 0).astype(BF)
            return carry

        lax.fori_loop(0, 32, one, 0)

    build_base()

    both(has["prev"], to_next.wait_recv)
    pack_rows(front, 0, 3)
    send_rows(1)
    both(has["next"], to_prev.wait_recv)
    pack_rows(back, 3 + planes, 3)
    send_rows(2)

    build_toeplitz()
    ku[...] = spread_rows(up[...])
    kd[...] = spread_rows(down[...])
    for k in range(3):
        kt[:, k * 256 : (k + 1) * 256] = spread_rows(tap[k])

    for k in range(3):
        both(has["below"], rows[k][0].wait_recv)
        both(has["above"], rows[k][1].wait_recv)

    per = 32 // GROUPS
    cols = [
        copy(xs.at[q * per : (q + 1) * per], xh.at[q * per : (q + 1) * per],
             col_s.at[q], col_r.at[q], me, other)
        for q in range(GROUPS)
    ]
    small = iota((per // 2, 8, 128), 1)
    for q in range(GROUPS):
        for p in range(planes + 6):
            ref, i = (front, p) if p < 3 else (vol, p - 3) if p < 3 + planes else (back, p - 3 - planes)
            own = ref[i, q * per * 8 : (q + 1) * per * 8].astype(F32).reshape(per // 2, 2, 8, 128)
            lo = belo[p, q * per * 4 : (q + 1) * per * 4].astype(F32).reshape(per // 2, 8, 128)
            hi = abov[p, q * per * 4 : (q + 1) * per * 4].astype(F32).reshape(per // 2, 8, 128)
            a = jnp.where(small < 4, lo, pltpu.roll(hi, 4, 1))
            b = jnp.where(small < 4, pltpu.roll(lo, 4, 1), hi)
            for j in range(per // 2):
                c = q * per + 2 * j
                xs[c, p * 16 : (p + 1) * 16] = jnp.concatenate([own[j, 0], a[j]], 0).astype(BF)
                xs[c + 1, p * 16 : (p + 1) * 16] = jnp.concatenate([own[j, 1], b[j]], 0).astype(BF)
        cols[q].start()

    depth_rows = 16 * (planes + 6)

    def outer(x, n):
        lane = iota((n, 128), 1)
        keep = (lane < 3 + 125 * t) & (lane >= 125 * t)
        return jnp.where(keep, x.astype(F32), 0.0).astype(BF)

    for q in range(GROUPS):
        cols[q].wait_recv()

        def conv(c, carry):
            cells = jnp.concatenate([xs[c], outer(xh[c], depth_rows)], 1)
            part = dot(toep[c, :, 0:128], cells[0:128]) + dot(
                toep[c, :, 128:depth_rows], cells[128:depth_rows]
            )
            total = shift_sum(part[:, 0:128], part[:, 128:256], 7, 48)
            for p in range(planes):
                spread[p, pl.ds(pl.multiple_of(c * 8, 8), 8)] = total[p * 8 : (p + 1) * 8]
            return carry

        lax.fori_loop(q * per, (q + 1) * per, conv, 0)

    def mix(p):
        s = spread[p].reshape(32, 8, 128)
        square = jnp.sum(s * s, axis=0) * (1.0 / 32)
        normed = (s * lax.rsqrt(square + 1e-05)[None]).reshape(256, 128).astype(BF)
        hidden = gelu(dot(ku[...], normed)).astype(BF)
        mixed[p + 1] = (vol[p].astype(F32) + dot(kd[...], hidden)).astype(BF)

    mix_next = copy(mixed.at[planes], mixed.at[0], mix_s.at[0], mix_r.at[0], me + bands, t)
    mix_prev = copy(mixed.at[1], mixed.at[planes + 1], mix_s.at[1], mix_r.at[1], me - bands, t)

    @pl.when(jnp.logical_not(has["prev"]))
    def _():
        mixed[0] = jnp.zeros((256, 128), BF)

    @pl.when(jnp.logical_not(has["next"]))
    def _():
        mixed[planes + 1] = jnp.zeros((256, 128), BF)

    def edge(i, carry):
        mix(i * (planes - 1))
        return carry

    lax.fori_loop(0, 2, edge, 0)
    both(has["next"], mix_next.start)
    both(has["prev"], mix_prev.start)

    def inner(p, carry):
        mix(p)
        return carry

    lax.fori_loop(1, planes - 1, inner, 0)
    both(has["prev"], mix_next.wait_recv)
    both(has["next"], mix_prev.wait_recv)

    scale = 4.0 / (planes * slabs)
    light = jnp.ones((8, 128), F32)
    color[...] = jnp.zeros((256, 128), F32)
    for p in range(planes):
        glow = dot(kt[...], mixed[p : p + 3].reshape(768, 128)).reshape(32, 8, 128)
        logit = opacity[0] * glow[0]
        for c in range(1, 32):
            logit = logit + opacity[c] * glow[c]
        alpha = scale / (1.0 + jnp.exp(-logit))
        color[...] += ((light * alpha)[None] * glow).reshape(256, 128)
        light = light * (1.0 - alpha)
    for h in range(8):
        pieces[h, 0:32] = color[pl.ds(h, 32, stride=8), :]
        pieces[h, 32:40] = jnp.broadcast_to(light[h : h + 1], (8, 128))

    sent = []
    for j in range(slabs):
        owner = band * slabs + j
        send = copy(pieces.at[j * r : (j + 1) * r], gathered.at[slab],
                    comp_s.at[j], comp_r.at[slab], owner, t)
        both(owner != me, send.start)
        sent.append((owner, send))

        @pl.when(owner == me)
        def _(j=j):
            gathered[slab] = pieces[j * r : (j + 1) * r]

    for s in range(slabs):
        src = s * bands + my_band
        take = copy(pieces.at[0:r], gathered.at[s], comp_s.at[0], comp_r.at[s], me, other)
        both(src != me, take.wait_recv)

    for y in range(r):
        image = gathered[0, y, 0:32]
        light_y = gathered[0, y, 32:33]
        for s in range(1, slabs):
            image = image + light_y * gathered[s, y, 0:32]
            light_y = light_y * gathered[s, y, 32:33]
        square = jnp.sum(image * image, axis=0, keepdims=True) * (1.0 / 32)
        flat[y] = (image * lax.rsqrt(square + 1e-05)).astype(BF)

    def img(slot, position, tile):
        return copy(flat, near.at[slot], img_s.at[slot], img_r.at[slot], position, tile)

    halo = [
        ("after", "before", img(0, me + 1, t)), ("before", "after", img(1, me - 1, t)),
        (None, None, img(2, me, other)),
        ("after", "before", img(3, me + 1, other)), ("before", "after", img(4, me - 1, other)),
    ]
    for to, _, c in halo:
        if to is None:
            c.start()
        else:
            both(has[to], c.start)
    for slot in (0, 3):
        both(jnp.logical_not(has["before"]), lambda slot=slot: zero(near.at[slot]))
    for slot in (1, 4):
        both(jnp.logical_not(has["after"]), lambda slot=slot: zero(near.at[slot]))
    for _, frm, c in halo:
        if frm is None:
            c.wait_recv()
        else:
            both(has[frm], c.wait_recv)

    lines = [jnp.concatenate([near[0, r - 1], outer(near[3, r - 1], 32)], 1)]
    for y in range(r):
        lines.append(jnp.concatenate([flat[y], outer(near[2, y], 32)], 1))
    lines.append(jnp.concatenate([near[1, 0], outer(near[4, 0], 32)], 1))
    for y in range(r):
        part = dot(dec[...], jnp.concatenate(lines[y : y + 3], 0))
        decoded = gelu(shift_sum(part[:, 0:128], part[:, 128:256], 3, 32)).astype(BF)
        values = dot(outw[...], decoded)
        for o in range(3):
            rgb[o, y : y + 1] = values[o : o + 1]

    both(has["next"], to_next.wait_send)
    both(has["prev"], to_prev.wait_send)
    for k in range(3):
        both(has["above"], rows[k][0].wait_send)
        both(has["below"], rows[k][1].wait_send)
    for q in range(GROUPS):
        cols[q].wait_send()
    both(has["next"], mix_next.wait_send)
    both(has["prev"], mix_prev.wait_send)
    for owner, send in sent:
        both(owner != me, send.wait_send)
    for to, _, c in halo:
        if to is None:
            c.wait_send()
        else:
            both(has[to], c.wait_send)


def body(
    volume, dw_weight, up_weight, down_weight, tap_weight, opacity_weight, decode_weight, out_weight
):
    planes = volume.shape[1]
    count = lax.axis_size("depth")
    bands = max(2, count // 8)
    slabs = count // bands
    r = 8 // slabs
    vol = volume.reshape(planes, 256, 128)
    taps = jnp.pad(jnp.transpose(dw_weight, (3, 0, 1, 2)).reshape(224, 49), ((0, 0), (0, 15)))
    dec = jnp.transpose(decode_weight, (3, 0, 2, 1)).reshape(96, 96)
    outw = jnp.pad(out_weight, ((0, 13), (0, 0)))
    all_planes = planes + 6
    vmem = pl.BlockSpec(memory_space=pltpu.VMEM)
    smem = pl.BlockSpec(memory_space=pltpu.SMEM)
    dma = pltpu.SemaphoreType.DMA
    return pl.pallas_call(
        functools.partial(kernel, bands, slabs),
        out_shape=jax.ShapeDtypeStruct((3, r, 128), F32),
        in_specs=[vmem, vmem, vmem, vmem, vmem, smem, vmem, vmem],
        out_specs=vmem,
        scratch_shapes=[
            pltpu.VMEM((3, 256, 128), BF), pltpu.VMEM((3, 256, 128), BF),
            pltpu.VMEM((all_planes, 128, 128), BF), pltpu.VMEM((all_planes, 128, 128), BF),
            pltpu.VMEM((all_planes, 128, 128), BF), pltpu.VMEM((all_planes, 128, 128), BF),
            pltpu.VMEM((8 * 224, 128), F32),
            pltpu.VMEM((32, 336, 256), BF),
            pltpu.VMEM((32, 16 * all_planes, 128), BF), pltpu.VMEM((32, 16 * all_planes, 128), BF),
            pltpu.VMEM((planes, 256, 128), F32),
            pltpu.VMEM((1024, 256), BF), pltpu.VMEM((256, 1024), BF), pltpu.VMEM((256, 768), BF),
            pltpu.VMEM((planes + 2, 256, 128), BF),
            pltpu.VMEM((256, 128), F32),
            pltpu.VMEM((8, 40, 128), F32), pltpu.VMEM((slabs, r, 40, 128), F32),
            pltpu.VMEM((r, 32, 128), BF), pltpu.VMEM((5, r, 32, 128), BF),
            dma((2,)), dma((2,)), dma((2, 3)), dma((2, 3)), dma((GROUPS,)), dma((GROUPS,)),
            dma((2,)), dma((2,)), dma((slabs,)), dma((slabs,)), dma((5,)), dma((5,)),
        ],
        compiler_params=pltpu.CompilerParams(
            collective_id=0, has_side_effects=True, vmem_limit_bytes=40 * 1024 * 1024
        ),
    )(vol, taps, up_weight, down_weight, tap_weight, opacity_weight, dec, outw)


def solution(mesh):
    in_specs = (P("depth", None, "group", None, "tile"), P(), P(), P(), P(), P(), P(), P())
    out_specs = P("group", "depth", "tile")
    return jax.shard_map(body, mesh=mesh, in_specs=in_specs, out_specs=out_specs, check_vma=False)
```

```python
import functools

import jax
import jax.numpy as jnp
from jax import lax
from jax.experimental import pallas as pl
from jax.experimental.pallas import tpu as pltpu
from jax.sharding import PartitionSpec as P

BF = jnp.bfloat16
F32 = jnp.float32
GROUPS = 4
UNROLL = 8


def iota(shape, dim):
    return lax.broadcasted_iota(jnp.int32, shape, dim)


def dot(a, b):
    return jnp.dot(a, b, preferred_element_type=F32)


def gelu(x):
    return 0.5 * x * (1.0 + jnp.tanh(0.7978845608028654 * (x + 0.044715 * (x * x * x))))


def spread_rows(weight, turned=False):
    m, n = weight.shape[::-1] if turned else weight.shape
    left = ((iota((8 * m, m), 0) >> 3) == iota((8 * m, m), 1)).astype(F32).astype(BF)
    right = (iota((n, 8 * n), 0) == (iota((n, 8 * n), 1) >> 3)).astype(F32).astype(BF)
    first = lax.dot_general(
        left, weight, (((1,), (1 if turned else 0,)), ((), ())), preferred_element_type=F32
    )
    full = dot(first.astype(BF), right)
    same = (iota(full.shape, 0) & 7) == (iota(full.shape, 1) & 7)
    return jnp.where(same, full, 0.0).astype(BF)


def shift_sum(main, halo, taps, rows):
    lane = iota((rows, 128), 1)
    total = None
    for k in range(taps):
        s = k - taps // 2
        m = main[k * rows : (k + 1) * rows]
        if s:
            h = halo[k * rows : (k + 1) * rows]
            pick = lane < s if s > 0 else lane >= 128 + s
            m = pltpu.roll(jnp.where(pick, h, m), (128 - s) % 128, 1)
        total = m if total is None else total + m
    return total


def kernel(
    bands, slabs,
    vol, taps, up, down, tap, opacity, dec, outw,
    rgb,
    front, back, upo, dno, belo, abov, base, toep, xs, xh, spread, ku, kd, kt,
    mixed, color, pieces, gathered, flat, near,
    plane_s, plane_r, row_s, row_r, col_s, col_r, mix_s, mix_r, comp_s, comp_r, img_s, img_r,
):
    planes = vol.shape[0]
    g = lax.axis_index("group")
    me = lax.axis_index("depth")
    t = lax.axis_index("tile")
    slab, band = me // bands, me % bands
    count = bands * slabs
    r = 8 // slabs
    other = 1 - t

    def at(position, tile):
        return (g, position, tile)

    has = {
        "next": slab < slabs - 1, "prev": slab > 0,
        "below": band < bands - 1, "above": band > 0,
        "after": me < count - 1, "before": me > 0,
    }
    bar = pltpu.get_barrier_semaphore()

    def greet(position, tile):
        pl.semaphore_signal(
            bar, inc=1, device_id=at(position, tile), device_id_type=pl.DeviceIdType.MESH
        )

    def both(cond, fn):
        pl.when(cond)(fn)

    greet(me, other)
    both(has["next"], lambda: greet(me + bands, t))
    both(has["prev"], lambda: greet(me - bands, t))
    both(has["below"], lambda: greet(me + 1, t))
    both(has["above"], lambda: greet(me - 1, t))
    for q in range(2):
        tile = t if q == 0 else other
        both(has["after"], lambda tile=tile: greet(me + 1, tile))
        both(has["before"], lambda tile=tile: greet(me - 1, tile))
    my_band, my_piece = me // slabs, me % slabs
    for s in range(slabs):
        src = s * bands + my_band
        both(src != me, lambda src=src: greet(src, t))
    one, two = jnp.int32(1), jnp.int32(2)
    total = one
    for name, amount in (("next", one), ("prev", one), ("below", one), ("above", one),
                         ("after", two), ("before", two)):
        total = total + jnp.where(has[name], amount, 0)
    for j in range(slabs):
        total = total + jnp.where(band * slabs + j != me, one, 0)
    pl.semaphore_wait(bar, total)

    def copy(src, dst, ss, rs, position, tile):
        return pltpu.make_async_remote_copy(
            src_ref=src, dst_ref=dst, send_sem=ss, recv_sem=rs,
            device_id=at(position, tile), device_id_type=pl.DeviceIdType.MESH,
        )

    def zero(ref):
        ref[...] = jnp.zeros(ref.shape, ref.dtype)

    to_next = copy(vol.at[planes - 3 : planes], front, plane_s.at[0], plane_r.at[0], me + bands, t)
    to_prev = copy(vol.at[0:3], back, plane_s.at[1], plane_r.at[1], me - bands, t)
    both(has["next"], to_next.start)
    both(has["prev"], to_prev.start)

    sub = iota((16, 8, 128), 1)

    def pack_rows(ref, start, n):
        def one(i, carry):
            x = ref[i].astype(F32).reshape(16, 2, 8, 128)
            a, b = x[:, 0], x[:, 1]
            low = jnp.where(sub < 4, a, pltpu.roll(b, 4, 1))
            high = jnp.where(sub < 4, pltpu.roll(a, 4, 1), b)
            upo[start + i] = low.reshape(128, 128).astype(BF)
            dno[start + i] = high.reshape(128, 128).astype(BF)
            return carry

        lax.fori_loop(0, n, one, 0)

    def row_copies(k, start, n):
        return (
            copy(upo.at[start : start + n], belo.at[start : start + n],
                 row_s.at[0, k], row_r.at[0, k], me - 1, t),
            copy(dno.at[start : start + n], abov.at[start : start + n],
                 row_s.at[1, k], row_r.at[1, k], me + 1, t),
        )

    rows = [row_copies(0, 3, planes), row_copies(1, 0, 3), row_copies(2, 3 + planes, 3)]

    def send_rows(k):
        both(has["above"], rows[k][0].start)
        both(has["below"], rows[k][1].start)

    pack_rows(vol, 3, planes)
    send_rows(0)
    both(jnp.logical_not(has["prev"]), lambda: zero(front))
    both(jnp.logical_not(has["next"]), lambda: zero(back))
    both(jnp.logical_not(has["below"]), lambda: zero(belo))
    both(jnp.logical_not(has["above"]), lambda: zero(abov))

    def build_base():
        for h in range(8):
            row, lane = iota((64, 128), 0), iota((64, 128), 1)
            dh = ((lane & 15) - h + 3) & 15
            hit = (row == (lane >> 4) * 7 + dh) & (dh < 7) & (lane < 112)
            base[h * 224 : (h + 1) * 224] = dot(taps[...], hit.astype(F32).astype(BF))

    def build_toeplitz():
        lane = iota((8, 128), 1)

        def one(c, carry):
            for k in range(7):
                b = base[pl.ds(k * 32 + c, 8, stride=224), :]
                low, high = [], []
                for p in range(planes):
                    moved = pltpu.roll(b, 16 * p, 1) if p else b
                    low.append(jnp.where(lane >= 16 * p, moved, 0.0))
                    high.append(jnp.where(lane < 16 * p, moved, 0.0))
                toep[c, k * 48 : (k + 1) * 48, 0:128] = jnp.concatenate(low, 0).astype(BF)
                toep[c, k * 48 : (k + 1) * 48, 128:256] = jnp.concatenate(high, 0).astype(BF)
            return carry

        lax.fori_loop(0, 32, one, 0)

    build_base()

    both(has["prev"], to_next.wait_recv)
    pack_rows(front, 0, 3)
    send_rows(1)
    both(has["next"], to_prev.wait_recv)
    pack_rows(back, 3 + planes, 3)
    send_rows(2)

    build_toeplitz()
    ku[...] = spread_rows(up[...], True)
    kd[...] = spread_rows(down[...])
    for k in range(3):
        kt[:, k * 256 : (k + 1) * 256] = spread_rows(tap[k])

    for k in range(3):
        both(has["below"], rows[k][0].wait_recv)
        both(has["above"], rows[k][1].wait_recv)

    per = 32 // GROUPS
    cols = [
        copy(xs.at[q * per : (q + 1) * per], xh.at[q * per : (q + 1) * per],
             col_s.at[q], col_r.at[q], me, other)
        for q in range(GROUPS)
    ]
    small = iota((per // 2, 8, 128), 1)
    for q in range(GROUPS):
        for p in range(planes + 6):
            ref, i = (front, p) if p < 3 else (vol, p - 3) if p < 3 + planes else (back, p - 3 - planes)
            own = ref[i, q * per * 8 : (q + 1) * per * 8].astype(F32).reshape(per // 2, 2, 8, 128)
            lo = belo[p, q * per * 4 : (q + 1) * per * 4].astype(F32).reshape(per // 2, 8, 128)
            hi = abov[p, q * per * 4 : (q + 1) * per * 4].astype(F32).reshape(per // 2, 8, 128)
            a = jnp.where(small < 4, lo, pltpu.roll(hi, 4, 1))
            b = jnp.where(small < 4, pltpu.roll(lo, 4, 1), hi)
            for j in range(per // 2):
                c = q * per + 2 * j
                xs[c, p * 16 : (p + 1) * 16] = jnp.concatenate([own[j, 0], a[j]], 0).astype(BF)
                xs[c + 1, p * 16 : (p + 1) * 16] = jnp.concatenate([own[j, 1], b[j]], 0).astype(BF)
        cols[q].start()

    depth_rows = 16 * (planes + 6)

    def outer(x, n):
        lane = iota((n, 128), 1)
        keep = (lane < 3 + 125 * t) & (lane >= 125 * t)
        return jnp.where(keep, x.astype(F32), 0.0).astype(BF)

    for q in range(GROUPS):
        cols[q].wait_recv()

        def conv(c, carry):
            cells = jnp.concatenate([xs[c], outer(xh[c], depth_rows)], 1)
            part = dot(toep[c, :, 0:depth_rows], cells)
            total = shift_sum(part[:, 0:128], part[:, 128:256], 7, 48)
            for p in range(planes):
                spread[p, pl.ds(pl.multiple_of(c * 8, 8), 8)] = total[p * 8 : (p + 1) * 8]
            return carry

        lax.fori_loop(q * per, (q + 1) * per, conv, 0, unroll=UNROLL)

    def mix(p):
        s = spread[p].reshape(32, 8, 128)
        square = jnp.sum(s * s, axis=0) * (1.0 / 32)
        normed = (s * lax.rsqrt(square + 1e-05)[None]).reshape(256, 128).astype(BF)
        hidden = gelu(dot(ku[...], normed)).astype(BF)
        mixed[p + 1] = (vol[p].astype(F32) + dot(kd[...], hidden)).astype(BF)

    mix_next = copy(mixed.at[planes], mixed.at[0], mix_s.at[0], mix_r.at[0], me + bands, t)
    mix_prev = copy(mixed.at[1], mixed.at[planes + 1], mix_s.at[1], mix_r.at[1], me - bands, t)

    @pl.when(jnp.logical_not(has["prev"]))
    def _():
        mixed[0] = jnp.zeros((256, 128), BF)

    @pl.when(jnp.logical_not(has["next"]))
    def _():
        mixed[planes + 1] = jnp.zeros((256, 128), BF)

    def edge(i, carry):
        mix(i * (planes - 1))
        return carry

    lax.fori_loop(0, 2, edge, 0, unroll=2)
    both(has["next"], mix_next.start)
    both(has["prev"], mix_prev.start)

    def inner(p, carry):
        mix(p)
        return carry

    lax.fori_loop(1, planes - 1, inner, 0, unroll=2)
    both(has["prev"], mix_next.wait_recv)
    both(has["next"], mix_prev.wait_recv)

    scale = 4.0 / (planes * slabs)
    light = jnp.ones((8, 128), F32)
    color[...] = jnp.zeros((256, 128), F32)
    for p in range(planes):
        glow = dot(kt[...], mixed[p : p + 3].reshape(768, 128)).reshape(32, 8, 128)
        logit = opacity[0] * glow[0]
        for c in range(1, 32):
            logit = logit + opacity[c] * glow[c]
        alpha = scale / (1.0 + jnp.exp(-logit))
        color[...] += ((light * alpha)[None] * glow).reshape(256, 128)
        light = light * (1.0 - alpha)
    for h in range(8):
        pieces[h, 0:32] = color[pl.ds(h, 32, stride=8), :]
        pieces[h, 32:40] = jnp.broadcast_to(light[h : h + 1], (8, 128))

    sent = []
    for j in range(slabs):
        owner = band * slabs + j
        send = copy(pieces.at[j * r : (j + 1) * r], gathered.at[slab],
                    comp_s.at[j], comp_r.at[slab], owner, t)
        both(owner != me, send.start)
        sent.append((owner, send))

        @pl.when(owner == me)
        def _(j=j):
            gathered[slab] = pieces[j * r : (j + 1) * r]

    for s in range(slabs):
        src = s * bands + my_band
        take = copy(pieces.at[0:r], gathered.at[s], comp_s.at[0], comp_r.at[s], me, other)
        both(src != me, take.wait_recv)

    for y in range(r):
        image = gathered[0, y, 0:32]
        light_y = gathered[0, y, 32:33]
        for s in range(1, slabs):
            image = image + light_y * gathered[s, y, 0:32]
            light_y = light_y * gathered[s, y, 32:33]
        square = jnp.sum(image * image, axis=0, keepdims=True) * (1.0 / 32)
        flat[y] = (image * lax.rsqrt(square + 1e-05)).astype(BF)

    def img(slot, position, tile):
        return copy(flat, near.at[slot], img_s.at[slot], img_r.at[slot], position, tile)

    halo = [
        ("after", "before", img(0, me + 1, t)), ("before", "after", img(1, me - 1, t)),
        (None, None, img(2, me, other)),
        ("after", "before", img(3, me + 1, other)), ("before", "after", img(4, me - 1, other)),
    ]
    for to, _, c in halo:
        if to is None:
            c.start()
        else:
            both(has[to], c.start)
    for slot in (0, 3):
        both(jnp.logical_not(has["before"]), lambda slot=slot: zero(near.at[slot]))
    for slot in (1, 4):
        both(jnp.logical_not(has["after"]), lambda slot=slot: zero(near.at[slot]))
    for _, frm, c in halo:
        if frm is None:
            c.wait_recv()
        else:
            both(has[frm], c.wait_recv)

    lines = [jnp.concatenate([near[0, r - 1], outer(near[3, r - 1], 32)], 1)]
    for y in range(r):
        lines.append(jnp.concatenate([flat[y], outer(near[2, y], 32)], 1))
    lines.append(jnp.concatenate([near[1, 0], outer(near[4, 0], 32)], 1))
    for y in range(r):
        part = dot(dec[0], lines[y]) + dot(dec[1], lines[y + 1]) + dot(dec[2], lines[y + 2])
        decoded = gelu(shift_sum(part[:, 0:128], part[:, 128:256], 3, 32)).astype(BF)
        values = dot(outw[...], decoded)
        for o in range(3):
            rgb[o, y : y + 1] = values[o : o + 1]

    both(has["next"], to_next.wait_send)
    both(has["prev"], to_prev.wait_send)
    for k in range(3):
        both(has["above"], rows[k][0].wait_send)
        both(has["below"], rows[k][1].wait_send)
    for q in range(GROUPS):
        cols[q].wait_send()
    both(has["next"], mix_next.wait_send)
    both(has["prev"], mix_prev.wait_send)
    for owner, send in sent:
        both(owner != me, send.wait_send)
    for to, _, c in halo:
        if to is None:
            c.wait_send()
        else:
            both(has[to], c.wait_send)


def body(
    volume, dw_weight, up_weight, down_weight, tap_weight, opacity_weight, decode_weight, out_weight
):
    planes = volume.shape[1]
    count = lax.axis_size("depth")
    bands = max(2, count // 8)
    slabs = count // bands
    r = 8 // slabs
    vol = volume.reshape(planes, 256, 128)
    taps = jnp.pad(jnp.transpose(dw_weight, (3, 0, 1, 2)).reshape(224, 49), ((0, 0), (0, 15)))
    dec = jnp.transpose(decode_weight, (2, 3, 0, 1)).reshape(3, 96, 32)
    all_planes = planes + 6
    vmem = pl.BlockSpec(memory_space=pltpu.VMEM)
    smem = pl.BlockSpec(memory_space=pltpu.SMEM)
    dma = pltpu.SemaphoreType.DMA
    return pl.pallas_call(
        functools.partial(kernel, bands, slabs),
        out_shape=jax.ShapeDtypeStruct((3, r, 128), F32),
        in_specs=[vmem, vmem, vmem, vmem, vmem, smem, vmem, vmem],
        out_specs=vmem,
        scratch_shapes=[
            pltpu.VMEM((3, 256, 128), BF), pltpu.VMEM((3, 256, 128), BF),
            pltpu.VMEM((all_planes, 128, 128), BF), pltpu.VMEM((all_planes, 128, 128), BF),
            pltpu.VMEM((all_planes, 128, 128), BF), pltpu.VMEM((all_planes, 128, 128), BF),
            pltpu.VMEM((8 * 224, 128), F32),
            pltpu.VMEM((32, 336, 256), BF),
            pltpu.VMEM((32, 16 * all_planes, 128), BF), pltpu.VMEM((32, 16 * all_planes, 128), BF),
            pltpu.VMEM((planes, 256, 128), F32),
            pltpu.VMEM((1024, 256), BF), pltpu.VMEM((256, 1024), BF), pltpu.VMEM((256, 768), BF),
            pltpu.VMEM((planes + 2, 256, 128), BF),
            pltpu.VMEM((256, 128), F32),
            pltpu.VMEM((8, 40, 128), F32), pltpu.VMEM((slabs, r, 40, 128), F32),
            pltpu.VMEM((r, 32, 128), BF), pltpu.VMEM((5, r, 32, 128), BF),
            dma((2,)), dma((2,)), dma((2, 3)), dma((2, 3)), dma((GROUPS,)), dma((GROUPS,)),
            dma((2,)), dma((2,)), dma((slabs,)), dma((slabs,)), dma((5,)), dma((5,)),
        ],
        compiler_params=pltpu.CompilerParams(
            collective_id=0, has_side_effects=True, vmem_limit_bytes=40 * 1024 * 1024
        ),
    )(vol, taps, up_weight.T, down_weight, tap_weight, opacity_weight, dec, out_weight)


def solution(mesh):
    in_specs = (P("depth", None, "group", None, "tile"), P(), P(), P(), P(), P(), P(), P())
    out_specs = P("group", "depth", "tile")
    return jax.shard_map(body, mesh=mesh, in_specs=in_specs, out_specs=out_specs, check_vma=False)
```

```python
import functools

import jax
import jax.numpy as jnp
from jax import lax
from jax.experimental import pallas as pl
from jax.experimental.pallas import tpu as pltpu
from jax.sharding import PartitionSpec as P

BF = jnp.bfloat16
F32 = jnp.float32
GROUPS = 4
UNROLL = 8


def iota(shape, dim):
    return lax.broadcasted_iota(jnp.int32, shape, dim)


def dot(a, b):
    return jnp.dot(a, b, preferred_element_type=F32)


def gelu(x):
    return 0.5 * x * (1.0 + jnp.tanh(0.7978845608028654 * (x + 0.044715 * (x * x * x))))


def spread_rows(weight, turned=False):
    m, n = weight.shape[::-1] if turned else weight.shape
    left = ((iota((8 * m, m), 0) >> 3) == iota((8 * m, m), 1)).astype(F32).astype(BF)
    right = (iota((n, 8 * n), 0) == (iota((n, 8 * n), 1) >> 3)).astype(F32).astype(BF)
    first = lax.dot_general(
        left, weight, (((1,), (1 if turned else 0,)), ((), ())), preferred_element_type=F32
    )
    full = dot(first.astype(BF), right)
    same = (iota(full.shape, 0) & 7) == (iota(full.shape, 1) & 7)
    return jnp.where(same, full, 0.0).astype(BF)


def shift_sum(main, halo, taps, rows):
    lane = iota((rows, 128), 1)
    total = None
    for k in range(taps):
        s = k - taps // 2
        m = main[k * rows : (k + 1) * rows]
        if s:
            h = halo[k * rows : (k + 1) * rows]
            pick = lane < s if s > 0 else lane >= 128 + s
            m = pltpu.roll(jnp.where(pick, h, m), (128 - s) % 128, 1)
        total = m if total is None else total + m
    return total


def kernel(
    bands, slabs,
    vol, taps, up, down, tap, opacity, dec, outw,
    rgb,
    front, back, upo, dno, belo, abov, base, toep, xs, xh, spread, ku, kd, kt,
    mixed, color, pieces, gathered, flat, near,
    plane_s, plane_r, row_s, row_r, col_s, col_r, mix_s, mix_r, comp_s, comp_r, img_s, img_r,
):
    planes = vol.shape[0]
    g = lax.axis_index("group")
    me = lax.axis_index("depth")
    t = lax.axis_index("tile")
    slab, band = me // bands, me % bands
    count = bands * slabs
    r = 8 // slabs
    other = 1 - t

    def at(position, tile):
        return (g, position, tile)

    has = {
        "next": slab < slabs - 1, "prev": slab > 0,
        "below": band < bands - 1, "above": band > 0,
        "after": me < count - 1, "before": me > 0,
    }
    bar = pltpu.get_barrier_semaphore()

    def greet(position, tile):
        pl.semaphore_signal(
            bar, inc=1, device_id=at(position, tile), device_id_type=pl.DeviceIdType.MESH
        )

    def both(cond, fn):
        pl.when(cond)(fn)

    greet(me, other)
    both(has["next"], lambda: greet(me + bands, t))
    both(has["prev"], lambda: greet(me - bands, t))
    both(has["below"], lambda: greet(me + 1, t))
    both(has["above"], lambda: greet(me - 1, t))
    for q in range(2):
        tile = t if q == 0 else other
        both(has["after"], lambda tile=tile: greet(me + 1, tile))
        both(has["before"], lambda tile=tile: greet(me - 1, tile))
    my_band, my_piece = me // slabs, me % slabs
    for s in range(slabs):
        src = s * bands + my_band
        both(src != me, lambda src=src: greet(src, t))
    one, two = jnp.int32(1), jnp.int32(2)
    total = one
    for name, amount in (("next", one), ("prev", one), ("below", one), ("above", one),
                         ("after", two), ("before", two)):
        total = total + jnp.where(has[name], amount, 0)
    for j in range(slabs):
        total = total + jnp.where(band * slabs + j != me, one, 0)
    pl.semaphore_wait(bar, total)

    def copy(src, dst, ss, rs, position, tile):
        return pltpu.make_async_remote_copy(
            src_ref=src, dst_ref=dst, send_sem=ss, recv_sem=rs,
            device_id=at(position, tile), device_id_type=pl.DeviceIdType.MESH,
        )

    def zero(ref):
        ref[...] = jnp.zeros(ref.shape, ref.dtype)

    to_next = copy(vol.at[planes - 3 : planes], front, plane_s.at[0], plane_r.at[0], me + bands, t)
    to_prev = copy(vol.at[0:3], back, plane_s.at[1], plane_r.at[1], me - bands, t)
    both(has["next"], to_next.start)
    both(has["prev"], to_prev.start)

    sub = iota((16, 8, 128), 1)

    def pack_rows(ref, start, n):
        def one(i, carry):
            x = ref[i].astype(F32).reshape(16, 2, 8, 128)
            a, b = x[:, 0], x[:, 1]
            low = jnp.where(sub < 4, a, pltpu.roll(b, 4, 1))
            high = jnp.where(sub < 4, pltpu.roll(a, 4, 1), b)
            upo[start + i] = low.reshape(128, 128).astype(BF)
            dno[start + i] = high.reshape(128, 128).astype(BF)
            return carry

        lax.fori_loop(0, n, one, 0, unroll=3)

    def row_copies(k, start, n):
        return (
            copy(upo.at[start : start + n], belo.at[start : start + n],
                 row_s.at[0, k], row_r.at[0, k], me - 1, t),
            copy(dno.at[start : start + n], abov.at[start : start + n],
                 row_s.at[1, k], row_r.at[1, k], me + 1, t),
        )

    rows = [row_copies(0, 3, planes), row_copies(1, 0, 3), row_copies(2, 3 + planes, 3)]

    def send_rows(k):
        both(has["above"], rows[k][0].start)
        both(has["below"], rows[k][1].start)

    pack_rows(vol, 3, planes)
    send_rows(0)
    both(jnp.logical_not(has["prev"]), lambda: zero(front))
    both(jnp.logical_not(has["next"]), lambda: zero(back))
    both(jnp.logical_not(has["below"]), lambda: zero(belo))
    both(jnp.logical_not(has["above"]), lambda: zero(abov))

    def build_base():
        for h in range(8):
            row, lane = iota((64, 128), 0), iota((64, 128), 1)
            dh = ((lane & 15) - h + 3) & 15
            hit = (row == (lane >> 4) * 7 + dh) & (dh < 7) & (lane < 112)
            base[h * 224 : (h + 1) * 224] = dot(taps[...], hit.astype(F32).astype(BF))

    def build_toeplitz():
        lane = iota((8, 128), 1)

        def one(c, carry):
            for k in range(7):
                b = base[pl.ds(k * 32 + c, 8, stride=224), :]
                low, high = [], []
                for p in range(planes):
                    moved = pltpu.roll(b, 16 * p, 1) if p else b
                    low.append(jnp.where(lane >= 16 * p, moved, 0.0))
                    high.append(jnp.where(lane < 16 * p, moved, 0.0))
                toep[c, k * 48 : (k + 1) * 48, 0:128] = jnp.concatenate(low, 0).astype(BF)
                toep[c, k * 48 : (k + 1) * 48, 128:256] = jnp.concatenate(high, 0).astype(BF)
            return carry

        lax.fori_loop(0, 32, one, 0, unroll=2)

    build_base()
    build_toeplitz()
    ku[...] = spread_rows(up[...], True)
    kd[...] = spread_rows(down[...])
    for k in range(3):
        kt[:, k * 256 : (k + 1) * 256] = spread_rows(tap[k])

    both(has["prev"], to_next.wait_recv)
    pack_rows(front, 0, 3)
    send_rows(1)
    both(has["next"], to_prev.wait_recv)
    pack_rows(back, 3 + planes, 3)
    send_rows(2)

    for k in range(3):
        both(has["below"], rows[k][0].wait_recv)
        both(has["above"], rows[k][1].wait_recv)

    per = 32 // GROUPS
    cols = [
        copy(xs.at[q * per : (q + 1) * per], xh.at[q * per : (q + 1) * per],
             col_s.at[q], col_r.at[q], me, other)
        for q in range(GROUPS)
    ]
    small = iota((per // 2, 8, 128), 1)
    for q in range(GROUPS):
        for p in range(planes + 6):
            ref, i = (front, p) if p < 3 else (vol, p - 3) if p < 3 + planes else (back, p - 3 - planes)
            own = ref[i, q * per * 8 : (q + 1) * per * 8].astype(F32).reshape(per // 2, 2, 8, 128)
            lo = belo[p, q * per * 4 : (q + 1) * per * 4].astype(F32).reshape(per // 2, 8, 128)
            hi = abov[p, q * per * 4 : (q + 1) * per * 4].astype(F32).reshape(per // 2, 8, 128)
            a = jnp.where(small < 4, lo, pltpu.roll(hi, 4, 1))
            b = jnp.where(small < 4, pltpu.roll(lo, 4, 1), hi)
            for j in range(per // 2):
                c = q * per + 2 * j
                xs[c, p * 16 : (p + 1) * 16] = jnp.concatenate([own[j, 0], a[j]], 0).astype(BF)
                xs[c + 1, p * 16 : (p + 1) * 16] = jnp.concatenate([own[j, 1], b[j]], 0).astype(BF)
        cols[q].start()

    depth_rows = 16 * (planes + 6)

    def outer(x, n):
        lane = iota((n, 128), 1)
        keep = (lane < 3 + 125 * t) & (lane >= 125 * t)
        return jnp.where(keep, x.astype(F32), 0.0).astype(BF)

    for q in range(GROUPS):
        cols[q].wait_recv()

        def conv(c, carry):
            cells = jnp.concatenate([xs[c], outer(xh[c], depth_rows)], 1)
            part = dot(toep[c, :, 0:depth_rows], cells)
            total = shift_sum(part[:, 0:128], part[:, 128:256], 7, 48)
            for p in range(planes):
                spread[p, pl.ds(pl.multiple_of(c * 8, 8), 8)] = total[p * 8 : (p + 1) * 8]
            return carry

        lax.fori_loop(q * per, (q + 1) * per, conv, 0, unroll=UNROLL)

    def mix(p):
        s = spread[p].reshape(32, 8, 128)
        square = jnp.sum(s * s, axis=0) * (1.0 / 32)
        normed = (s * lax.rsqrt(square + 1e-05)[None]).reshape(256, 128).astype(BF)
        hidden = gelu(dot(ku[...], normed)).astype(BF)
        mixed[p + 1] = (vol[p].astype(F32) + dot(kd[...], hidden)).astype(BF)

    mix_next = copy(mixed.at[planes], mixed.at[0], mix_s.at[0], mix_r.at[0], me + bands, t)
    mix_prev = copy(mixed.at[1], mixed.at[planes + 1], mix_s.at[1], mix_r.at[1], me - bands, t)

    @pl.when(jnp.logical_not(has["prev"]))
    def _():
        mixed[0] = jnp.zeros((256, 128), BF)

    @pl.when(jnp.logical_not(has["next"]))
    def _():
        mixed[planes + 1] = jnp.zeros((256, 128), BF)

    def edge(i, carry):
        mix(i * (planes - 1))
        return carry

    lax.fori_loop(0, 2, edge, 0, unroll=2)
    both(has["next"], mix_next.start)
    both(has["prev"], mix_prev.start)

    def inner(p, carry):
        mix(p)
        return carry

    lax.fori_loop(1, planes - 1, inner, 0, unroll=2)

    def glow_of(p):
        return dot(kt[...], mixed[p : p + 3].reshape(768, 128)).reshape(32, 8, 128)

    glows = {p: glow_of(p) for p in range(1, planes - 1)}
    both(has["prev"], mix_next.wait_recv)
    both(has["next"], mix_prev.wait_recv)
    glows[0], glows[planes - 1] = glow_of(0), glow_of(planes - 1)

    scale = 4.0 / (planes * slabs)
    light = jnp.ones((8, 128), F32)
    color[...] = jnp.zeros((256, 128), F32)
    for p in range(planes):
        glow = glows[p]
        logit = opacity[0] * glow[0]
        for c in range(1, 32):
            logit = logit + opacity[c] * glow[c]
        alpha = scale / (1.0 + jnp.exp(-logit))
        color[...] += ((light * alpha)[None] * glow).reshape(256, 128)
        light = light * (1.0 - alpha)
    for h in range(8):
        pieces[h, 0:32] = color[pl.ds(h, 32, stride=8), :]
        pieces[h, 32:40] = jnp.broadcast_to(light[h : h + 1], (8, 128))

    sent = []
    for j in range(slabs):
        owner = band * slabs + j
        send = copy(pieces.at[j * r : (j + 1) * r], gathered.at[slab],
                    comp_s.at[j], comp_r.at[slab], owner, t)
        both(owner != me, send.start)
        sent.append((owner, send))

        @pl.when(owner == me)
        def _(j=j):
            gathered[slab] = pieces[j * r : (j + 1) * r]

    for s in range(slabs):
        src = s * bands + my_band
        take = copy(pieces.at[0:r], gathered.at[s], comp_s.at[0], comp_r.at[s], me, other)
        both(src != me, take.wait_recv)

    for y in range(r):
        image = gathered[0, y, 0:32]
        light_y = gathered[0, y, 32:33]
        for s in range(1, slabs):
            image = image + light_y * gathered[s, y, 0:32]
            light_y = light_y * gathered[s, y, 32:33]
        square = jnp.sum(image * image, axis=0, keepdims=True) * (1.0 / 32)
        flat[y] = (image * lax.rsqrt(square + 1e-05)).astype(BF)

    def img(slot, position, tile):
        return copy(flat, near.at[slot], img_s.at[slot], img_r.at[slot], position, tile)

    halo = [
        ("after", "before", img(0, me + 1, t)), ("before", "after", img(1, me - 1, t)),
        (None, None, img(2, me, other)),
        ("after", "before", img(3, me + 1, other)), ("before", "after", img(4, me - 1, other)),
    ]
    for to, _, c in halo:
        if to is None:
            c.start()
        else:
            both(has[to], c.start)
    for slot in (0, 3):
        both(jnp.logical_not(has["before"]), lambda slot=slot: zero(near.at[slot]))
    for slot in (1, 4):
        both(jnp.logical_not(has["after"]), lambda slot=slot: zero(near.at[slot]))
    for _, frm, c in halo:
        if frm is None:
            c.wait_recv()
        else:
            both(has[frm], c.wait_recv)

    lines = [jnp.concatenate([near[0, r - 1], outer(near[3, r - 1], 32)], 1)]
    for y in range(r):
        lines.append(jnp.concatenate([flat[y], outer(near[2, y], 32)], 1))
    lines.append(jnp.concatenate([near[1, 0], outer(near[4, 0], 32)], 1))
    for y in range(r):
        part = dot(dec[0], lines[y]) + dot(dec[1], lines[y + 1]) + dot(dec[2], lines[y + 2])
        decoded = gelu(shift_sum(part[:, 0:128], part[:, 128:256], 3, 32)).astype(BF)
        values = dot(outw[...], decoded)
        for o in range(3):
            rgb[o, y : y + 1] = values[o : o + 1]

    both(has["next"], to_next.wait_send)
    both(has["prev"], to_prev.wait_send)
    for k in range(3):
        both(has["above"], rows[k][0].wait_send)
        both(has["below"], rows[k][1].wait_send)
    for q in range(GROUPS):
        cols[q].wait_send()
    both(has["next"], mix_next.wait_send)
    both(has["prev"], mix_prev.wait_send)
    for owner, send in sent:
        both(owner != me, send.wait_send)
    for to, _, c in halo:
        if to is None:
            c.wait_send()
        else:
            both(has[to], c.wait_send)


def body(
    volume, dw_weight, up_weight, down_weight, tap_weight, opacity_weight, decode_weight, out_weight
):
    planes = volume.shape[1]
    count = lax.axis_size("depth")
    bands = max(2, count // 8)
    slabs = count // bands
    r = 8 // slabs
    vol = volume.reshape(planes, 256, 128)
    taps = jnp.pad(jnp.transpose(dw_weight, (3, 0, 1, 2)).reshape(224, 49), ((0, 0), (0, 15)))
    dec = jnp.transpose(decode_weight, (2, 3, 0, 1)).reshape(3, 96, 32)
    all_planes = planes + 6
    vmem = pl.BlockSpec(memory_space=pltpu.VMEM)
    smem = pl.BlockSpec(memory_space=pltpu.SMEM)
    dma = pltpu.SemaphoreType.DMA
    return pl.pallas_call(
        functools.partial(kernel, bands, slabs),
        out_shape=jax.ShapeDtypeStruct((3, r, 128), F32),
        in_specs=[vmem, vmem, vmem, vmem, vmem, smem, vmem, vmem],
        out_specs=vmem,
        scratch_shapes=[
            pltpu.VMEM((3, 256, 128), BF), pltpu.VMEM((3, 256, 128), BF),
            pltpu.VMEM((all_planes, 128, 128), BF), pltpu.VMEM((all_planes, 128, 128), BF),
            pltpu.VMEM((all_planes, 128, 128), BF), pltpu.VMEM((all_planes, 128, 128), BF),
            pltpu.VMEM((8 * 224, 128), F32),
            pltpu.VMEM((32, 336, 256), BF),
            pltpu.VMEM((32, 16 * all_planes, 128), BF), pltpu.VMEM((32, 16 * all_planes, 128), BF),
            pltpu.VMEM((planes, 256, 128), F32),
            pltpu.VMEM((1024, 256), BF), pltpu.VMEM((256, 1024), BF), pltpu.VMEM((256, 768), BF),
            pltpu.VMEM((planes + 2, 256, 128), BF),
            pltpu.VMEM((256, 128), F32),
            pltpu.VMEM((8, 40, 128), F32), pltpu.VMEM((slabs, r, 40, 128), F32),
            pltpu.VMEM((r, 32, 128), BF), pltpu.VMEM((5, r, 32, 128), BF),
            dma((2,)), dma((2,)), dma((2, 3)), dma((2, 3)), dma((GROUPS,)), dma((GROUPS,)),
            dma((2,)), dma((2,)), dma((slabs,)), dma((slabs,)), dma((5,)), dma((5,)),
        ],
        compiler_params=pltpu.CompilerParams(
            collective_id=0, has_side_effects=True, vmem_limit_bytes=40 * 1024 * 1024
        ),
    )(vol, taps, up_weight.T, down_weight, tap_weight, opacity_weight, dec, out_weight)


def solution(mesh):
    in_specs = (P("depth", None, "group", None, "tile"), P(), P(), P(), P(), P(), P(), P())
    out_specs = P("group", "depth", "tile")
    return jax.shard_map(body, mesh=mesh, in_specs=in_specs, out_specs=out_specs, check_vma=False)
```
